512 devices in a mesh: dp: 32 (over z, y_lo), tensor: 16 (over x, y_hi, core).
Axes of the slice: x: 4, y: 8 (y_hi: 2, y_lo: 4; y = y_hi * 4 + y_lo), z: 8, core: 2. Of those that a mesh axis runs over, the one named last changes fastest.
Arguments:
- activations: bfloat16 [2, 2048, 8192], P(None, 'dp'), may hold values from -6 to 6
- out_grads: bfloat16 [2, 2048, 8192], P(None, 'dp'), may hold values from -6 to 6
- act_basis: bfloat16 [8192, 6144], P('dp', 'tensor'), may hold values from -0.0625 to 0.0625
- grad_basis: bfloat16 [8192, 4096], P('dp', 'tensor'), may hold values from -0.0625 to 0.0625
Outputs:
- adjusted_spectrum: float32 [4096, 6144], P('tensor', 'dp')
The draws below stay inside these ranges and needn't reach their ends.
All inputs are finite; a program needn't handle non-finite values.
Results may differ from the reference program's by a relative error of at most 0.0041.
Values may be sent and summed in bfloat16 or wider, within the bound.
No kernel may reach another device: no remote copies, remote signals or barrier semaphores. Data moves between devices by JAX's collectives and lax.ppermute only.
A program may use at most 64 MiB of HBM per device.

```python
import jax
import jax.numpy as jnp

D = 8192
INPUT_SPECTRAL = 6144
BACKWARD_SPECTRAL = 4096
BATCH_STRINGS = 2
STRING_POSITIONS = 2048


def steps_of(rng, extent, split, low, top_value):
    gain, own = 1.0, jax.random.fold_in(rng, 6)
    for axis_at, shards_of in split:
        heights = jnp.exp(jax.random.uniform(jax.random.fold_in(own, axis_at), (shards_of,), jnp.float32, low / len(split), top_value / len(split)))
        gain = gain * jnp.repeat(heights, extent[axis_at] // shards_of).reshape([-1 if axis == axis_at else 1 for axis in range(len(extent))])
    return gain


def scatter_about(own_key, dims, width, limit, shards=(), kind=jnp.bfloat16):
    result = width * jax.random.normal(own_key, dims, jnp.float32)
    if shards:
        result = result * steps_of(own_key, dims, shards, -0.22, 0.18)
    return jnp.clip(result, -limit, limit).astype(kind)


def setup_inputs(seed: int = 0) -> dict:
    arg_keys = jax.random.split(jax.random.key(seed), 5)
    return {
        "activations": scatter_about(arg_keys[0], (BATCH_STRINGS, STRING_POSITIONS, D), 1.0, 6.0, ((1, 32),)),
        "out_grads": scatter_about(arg_keys[1], (BATCH_STRINGS, STRING_POSITIONS, D), 1.0, 6.0, ((1, 32),)),
        "act_basis": scatter_about(arg_keys[2], (D, INPUT_SPECTRAL), D ** -0.5, 0.0625, ((0, 32), (1, 16))),
        "grad_basis": scatter_about(arg_keys[3], (D, BACKWARD_SPECTRAL), D ** -0.5, 0.0625, ((0, 32), (1, 16))),
    }


def rotate(values, basis):
    flat = values.reshape(values.shape[0] * values.shape[1], values.shape[2])
    turned = jnp.dot(flat, basis, preferred_element_type=jnp.float32)
    return turned.astype(jnp.bfloat16).reshape(values.shape[0], values.shape[1], basis.shape[1])


def reference(activations, out_grads, act_basis, grad_basis):
    turned_acts = rotate(activations, act_basis)
    turned_grads = rotate(out_grads, grad_basis)
    adjusted_spectrum = jnp.zeros((BACKWARD_SPECTRAL, INPUT_SPECTRAL), jnp.float32)
    for sequence in range(BATCH_STRINGS):
        eigvec_outer = jnp.dot(turned_grads[sequence].T, turned_acts[sequence], preferred_element_type=jnp.float32)
        adjusted_spectrum = adjusted_spectrum + eigvec_outer * eigvec_outer
    return adjusted_spectrum / (BATCH_STRINGS * STRING_POSITIONS)
```

```python
import jax
import jax.numpy as jnp
from jax import lax
from jax.experimental import pallas as pl
from jax.experimental.pallas import tpu as pltpu
from jax.sharding import Mesh, PartitionSpec as P

Z, Y, X, H, C = "z", "y", "x", "h", "c"
NZ, NY, NX, NH, NC = 8, 4, 4, 2, 2

VMEM_LIMIT = 40 * 2**20
SCALARS = pl.BlockSpec(memory_space=pltpu.SMEM)
WHOLE = pl.BlockSpec(memory_space=pltpu.VMEM)


def swap_cores(v):
    return lax.ppermute(v, C, [(0, 1), (1, 0)])


def ring_y(v, shift):
    pairs = []
    for at in range(NH * NY):
        to = (at + shift) % (NH * NY)
        pairs.append((at % NY * NH + at // NY, to % NY * NH + to // NY))
    return lax.ppermute(v, (Y, H), pairs)


def transpose_planes(v):
    pairs = []
    for z in range(NZ):
        for t in range(NX * NH):
            pairs.append((z * NX * NH + t, t * NX * NH + z))
    return lax.ppermute(v, (Z, X, H), pairs)


def spread(v, axes, count):
    return lax.all_to_all(jnp.broadcast_to(v[None], (count,) + v.shape), axes, 0, 0)


def cut_kernel(at_ref, v_ref, own_ref, after_ref, before_ref, across_ref):
    y, core = at_ref[0], at_ref[1]
    width = own_ref.shape[2] // 2
    for z in range(2):
        for steps, out in ((0, own_ref), (1, after_ref), (3, before_ref), (2, across_ref)):
            block = z * NY + lax.rem(y + steps, NY)
            cols = pl.ds(pl.multiple_of(block * width, width), width)
            if steps == 0:
                out[:, :, z * width : (z + 1) * width] = v_ref[:, :, cols]
            else:
                out[:, z * width : (z + 1) * width] = v_ref[core, :, cols]


def cut_features(at, values):
    seqs, tokens, features = values.shape
    steps = NZ // 2
    part = features // NY // steps
    piece = jax.ShapeDtypeStruct((tokens, features // NY), values.dtype)
    piece_spec = pl.BlockSpec((tokens, part), lambda i: (0, i))
    return pl.pallas_call(
        cut_kernel,
        grid=(steps,),
        out_shape=(
            jax.ShapeDtypeStruct((seqs, tokens, features // NY), values.dtype),
            piece,
            piece,
            piece,
        ),
        in_specs=[SCALARS, pl.BlockSpec((seqs, tokens, part * NY), lambda i: (0, 0, i))],
        out_specs=(pl.BlockSpec((seqs, tokens, part), lambda i: (0, 0, i)),) + (piece_spec,) * 3,
        compiler_params=pltpu.CompilerParams(vmem_limit_bytes=VMEM_LIMIT),
    )(at, values)


def turn_kernel(at_ref, own_ref, *refs):
    *pieces, basis_ref, out_ref = refs
    y, core = at_ref[0], at_ref[1]
    tokens = own_ref.shape[1]
    rows = [own_ref[0], own_ref[1]] + [piece[...] for piece in pieces]
    product = jnp.dot(
        jnp.concatenate(rows, axis=0), basis_ref[...], preferred_element_type=jnp.float32
    )
    places = [(0, y), (1, y)]
    for seq in (core, 1 - core):
        places += [(seq, lax.rem(y + steps, NY)) for steps in (3, 1, 2)]
    for i, (seq, source) in enumerate(places):
        out_ref[seq, source] = product[i * tokens : (i + 1) * tokens]


def turn(at, own, pieces, basis):
    seqs, tokens, _ = own.shape
    cols = basis.shape[1]
    out = pl.pallas_call(
        turn_kernel,
        out_shape=jax.ShapeDtypeStruct((seqs, NY, tokens, cols), jnp.float32),
        in_specs=[SCALARS] + [WHOLE] * (2 + len(pieces)),
        out_specs=WHOLE,
        compiler_params=pltpu.CompilerParams(vmem_limit_bytes=VMEM_LIMIT),
    )(at, own, *pieces, basis)
    return out.reshape(NY, -1, cols)


def outer_kernel(at_ref, mine_ref, other_ref, grads_ref, out_ref):
    core = at_ref[1]
    grads = grads_ref[...]
    for acts, place in ((mine_ref, core), (other_ref, 1 - core)):
        product = lax.dot_general(
            acts[...], grads, (((0,), (0,)), ((), ())), preferred_element_type=jnp.float32
        )
        out_ref[place] = product.astype(out_ref.dtype)


def outer_product(at, mine, other, grads):
    out = pl.pallas_call(
        outer_kernel,
        out_shape=jax.ShapeDtypeStruct((NC, mine.shape[1], grads.shape[1]), jnp.bfloat16),
        in_specs=[SCALARS] + [WHOLE] * 3,
        out_specs=WHOLE,
        compiler_params=pltpu.CompilerParams(vmem_limit_bytes=VMEM_LIMIT),
    )(at, mine, other, grads)
    return out.reshape(NY, -1, grads.shape[1])


def move_tokens(at, values):
    own, to_after, to_before, to_across = cut_features(at, values)
    mine = [ring_y(to_after, 1), ring_y(to_before, -1), ring_y(to_across, 2)]
    return own, mine + [swap_cores(v) for v in mine]


def scatter_sum(parts):
    return jnp.sum(lax.all_to_all(parts, Y, 0, 0), axis=0).astype(jnp.bfloat16)


def local(activations, out_grads, act_basis, grad_basis):
    at = jnp.stack([lax.axis_index(Y), lax.axis_index(C)]).astype(jnp.int32)
    act_rows = lax.all_gather(act_basis, Z, axis=0, tiled=True)
    grad_rows = lax.all_gather(grad_basis, Z, axis=0, tiled=True)
    act_own, act_pieces = move_tokens(at, activations)
    grad_own, grad_pieces = move_tokens(at, out_grads)

    act_turned = scatter_sum(turn(at, act_own, act_pieces, act_rows))
    grad_turned = scatter_sum(turn(at, grad_own, grad_pieces, grad_rows))

    grad_panel = lax.all_gather(grad_turned, Z, axis=0, tiled=True)
    act_panel = spread(transpose_planes(act_turned), (X, H), NX * NH)
    act_panel = act_panel.reshape(-1, act_basis.shape[1])

    outer = outer_product(at, act_panel, swap_cores(act_panel), grad_panel)
    got = lax.all_to_all(outer, Y, 0, 0).astype(jnp.float32)
    first, second = got[0] + got[1], got[2] + got[3]
    count = activations.shape[0] * activations.shape[1] * NZ * NY
    return ((first * first + second * second) / count).T


def solution(mesh):
    fine = Mesh(mesh.devices.reshape(NZ, NY, NX, NH, NC), (Z, Y, X, H, C))
    dp, tensor = (Z, Y), (X, H, C)
    placed = (P(None, dp, None), P(None, dp, None), P(dp, tensor), P(dp, tensor))
    return jax.shard_map(
        local, mesh=fine, in_specs=placed, out_specs=P(tensor, dp), check_vma=False
    )
```

```python
import jax
import jax.numpy as jnp
from jax import lax
from jax.experimental import pallas as pl
from jax.experimental.pallas import tpu as pltpu
from jax.sharding import Mesh, PartitionSpec as P

Z, Y, X, H, C = "z", "y", "x", "h", "c"
NZ, NY, NX, NH, NC = 8, 4, 4, 2, 2

VMEM_LIMIT = 40 * 2**20
SCALARS = pl.BlockSpec(memory_space=pltpu.SMEM)
WHOLE = pl.BlockSpec(memory_space=pltpu.VMEM)


def swap_cores(v):
    return lax.ppermute(v, C, [(0, 1), (1, 0)])


def ring_y(v, shift):
    pairs = []
    for at in range(NH * NY):
        to = (at + shift(at)) % (NH * NY)
        pairs.append((at % NY * NH + at // NY, to % NY * NH + to // NY))
    return lax.ppermute(v, (Y, H), pairs)


def ring_z(v, shift):
    return lax.ppermute(v, Z, [(at, (at + shift(at)) % NZ) for at in range(NZ)])


def one_way(step):
    return lambda at: step


def either_way(at):
    return 2 if at % 2 == 0 else -2


def transpose_planes(v, flip):
    pairs = []
    for z in range(NZ):
        for t in range(NX * NH):
            pairs.append((z * NX * NH + t, t * NX * NH + (z ^ flip)))
    return lax.ppermute(v, (Z, X, H), pairs)


def gather_z(v, z):
    left1, right1 = ring_z(v, one_way(1)), ring_z(v, one_way(-1))
    left2, right2 = ring_z(v, one_way(2)), ring_z(v, one_way(-2))
    left3, right3 = ring_z(left2, one_way(1)), ring_z(right2, one_way(-1))
    far = ring_z(jnp.where(z % 2 == 0, left2, right2), either_way)
    return [v, left1, right1, left2, right2, left3, right3, far]


STEPS_Z = (0, 7, 1, 6, 2, 5, 3, 4)


def spread(v, axes, count):
    return lax.all_to_all(jnp.broadcast_to(v[None], (count,) + v.shape), axes, 0, 0)


def cut_kernel(at_ref, acts_ref, grads_ref, own_ref, after_ref, before_ref, across_ref):
    y, core = at_ref[0], at_ref[1]
    width = own_ref.shape[3] // 2
    for z in range(2):
        for steps, out in ((0, own_ref), (1, after_ref), (3, before_ref), (2, across_ref)):
            block = z * NY + lax.rem(y + steps, NY)
            cols = pl.ds(pl.multiple_of(block * width, width), width)
            for i, values in enumerate((acts_ref, grads_ref)):
                if steps == 0:
                    out[i, :, :, z * width : (z + 1) * width] = values[:, :, cols]
                else:
                    out[i, :, z * width : (z + 1) * width] = values[core, :, cols]


def cut_features(at, acts, grads):
    seqs, tokens, features = acts.shape
    steps = NZ // 2
    part = features // NY // steps
    whole_spec = pl.BlockSpec((seqs, tokens, part * NY), lambda i: (0, 0, i))
    piece = jax.ShapeDtypeStruct((2, tokens, features // NY), acts.dtype)
    piece_spec = pl.BlockSpec((2, tokens, part), lambda i: (0, 0, i))
    return pl.pallas_call(
        cut_kernel,
        grid=(steps,),
        out_shape=(
            jax.ShapeDtypeStruct((2, seqs, tokens, features // NY), acts.dtype),
            piece,
            piece,
            piece,
        ),
        in_specs=[SCALARS, whole_spec, whole_spec],
        out_specs=(pl.BlockSpec((2, seqs, tokens, part), lambda i: (0, 0, 0, i)),)
        + (piece_spec,) * 3,
        compiler_params=pltpu.CompilerParams(vmem_limit_bytes=VMEM_LIMIT),
    )(at, acts, grads)


def turn_kernel(which, at_ref, own_ref, *refs):
    pieces, basis_refs, (out_ref, rows_ref) = refs[:6], refs[6:-2], refs[-2:]
    y, core, z = at_ref[0], at_ref[1], at_ref[2]
    tokens = own_ref.shape[2]
    rows = [own_ref[which, 0], own_ref[which, 1]] + [piece[which] for piece in pieces]
    if len(basis_refs) == 1:
        basis = basis_refs[0][...]
    else:
        depth = basis_refs[0].shape[0]
        for steps, part in zip(STEPS_Z, basis_refs):
            start = lax.rem(z + steps, NZ) * depth
            rows_ref[pl.ds(pl.multiple_of(start, depth), depth)] = part[...]
        basis = rows_ref[...]
    product = jnp.dot(
        jnp.concatenate(rows, axis=0), basis, preferred_element_type=jnp.float32
    )
    places = [(0, y), (1, y)]
    for seq in (core, 1 - core):
        places += [(seq, lax.rem(y + steps, NY)) for steps in (3, 1, 2)]
    for i, (seq, source) in enumerate(places):
        out_ref[seq, source] = product[i * tokens : (i + 1) * tokens]


def turn(which, at, own, pieces, bases):
    _, seqs, tokens, features = own.shape
    cols = bases[0].shape[1]
    out = pl.pallas_call(
        lambda *refs: turn_kernel(which, *refs),
        out_shape=jax.ShapeDtypeStruct((seqs, NY, tokens, cols), jnp.float32),
        in_specs=[SCALARS] + [WHOLE] * (1 + len(pieces) + len(bases)),
        out_specs=WHOLE,
        scratch_shapes=[pltpu.VMEM((features, cols), own.dtype)],
        compiler_params=pltpu.CompilerParams(vmem_limit_bytes=VMEM_LIMIT),
    )(at, own, *pieces, *bases)
    return out.reshape(NY, -1, cols)


def outer_kernel(at_ref, mine_ref, other_ref, grads_ref, out_ref):
    core = at_ref[1]
    grads = grads_ref[...]
    for acts, place in ((mine_ref, core), (other_ref, 1 - core)):
        product = lax.dot_general(
            acts[...], grads, (((0,), (0,)), ((), ())), preferred_element_type=jnp.float32
        )
        out_ref[place] = product.astype(out_ref.dtype)


def outer_product(at, mine, other, grads):
    out = pl.pallas_call(
        outer_kernel,
        out_shape=jax.ShapeDtypeStruct((NC, mine.shape[1], grads.shape[1]), jnp.bfloat16),
        in_specs=[SCALARS] + [WHOLE] * 3,
        out_specs=WHOLE,
        compiler_params=pltpu.CompilerParams(vmem_limit_bytes=VMEM_LIMIT),
    )(at, mine, other, grads)
    return out.reshape(NY, -1, grads.shape[1])


def scatter_sum(parts):
    return jnp.sum(lax.all_to_all(parts, Y, 0, 0), axis=0).astype(jnp.bfloat16)


def local(activations, out_grads, act_basis, grad_basis):
    z, h = lax.axis_index(Z), lax.axis_index(H)
    at = jnp.stack([lax.axis_index(Y), lax.axis_index(C), z]).astype(jnp.int32)
    act_rows = lax.all_gather(act_basis, Z, axis=0, tiled=True)

    own, to_after, to_before, to_across = cut_features(at, activations, out_grads)
    pieces = [
        ring_y(to_after, one_way(1)),
        ring_y(to_before, one_way(-1)),
        ring_y(to_across, either_way),
    ]
    pieces += [swap_cores(v) for v in pieces]
    grad_rows = gather_z(grad_basis, z)

    grad_turned = scatter_sum(turn(1, at, own, pieces, grad_rows))
    act_turned = scatter_sum(turn(0, at, own, pieces, [act_rows]))

    grad_panel = spread(grad_turned, Z, NZ).reshape(-1, grad_basis.shape[1])
    near, far = transpose_planes(act_turned, 0), transpose_planes(act_turned, 1)
    pair = jnp.where(h == 0, jnp.stack([near, far]), jnp.stack([far, near]))
    act_panel = spread(pair, X, NX).reshape(-1, act_basis.shape[1])

    outer = outer_product(at, act_panel, swap_cores(act_panel), grad_panel)
    got = lax.all_to_all(outer, Y, 0, 0).astype(jnp.float32)
    first, second = got[0] + got[1], got[2] + got[3]
    count = activations.shape[0] * activations.shape[1] * NZ * NY
    return ((first * first + second * second) / count).T


def solution(mesh):
    fine = Mesh(mesh.devices.reshape(NZ, NY, NX, NH, NC), (Z, Y, X, H, C))
    dp, tensor = (Z, Y), (X, H, C)
    placed = (P(None, dp, None), P(None, dp, None), P(dp, tensor), P(dp, tensor))
    return jax.shard_map(
        local, mesh=fine, in_specs=placed, out_specs=P(tensor, dp), check_vma=False
    )
```

```python
import jax
import jax.numpy as jnp
from jax import lax
from jax.experimental import pallas as pl
from jax.experimental.pallas import tpu as pltpu
from jax.sharding import Mesh, PartitionSpec as P

Z, Y, X, H, C = "z", "y", "x", "h", "c"
NZ, NY, NX, NH, NC = 8, 4, 4, 2, 2

VMEM_LIMIT = 12 * 2**20
TURN_LIMIT = 60 * 2**20
SCALARS = pl.BlockSpec(memory_space=pltpu.SMEM)
WHOLE = pl.BlockSpec(memory_space=pltpu.VMEM)
IN_HBM = pl.BlockSpec(memory_space=pltpu.HBM)
ANY = pl.BlockSpec(memory_space=pl.ANY)


def swap_cores(v):
    return lax.ppermute(v, C, [(0, 1), (1, 0)])


def ring_y(v, shift):
    pairs = []
    for at in range(NH * NY):
        to = (at + shift(at)) % (NH * NY)
        pairs.append((at % NY * NH + at // NY, to % NY * NH + to // NY))
    return lax.ppermute(v, (Y, H), pairs)


def one_way(step):
    return lambda at: step


def either_way(at):
    return 2 if at % 2 == 0 else -2


def transpose_planes(v, flip):
    pairs = []
    for z in range(NZ):
        for t in range(NX * NH):
            pairs.append((z * NX * NH + t, t * NX * NH + (z ^ flip)))
    return lax.ppermute(v, (Z, X, H), pairs)


def spread(v, axes, count):
    return lax.all_to_all(jnp.broadcast_to(v[None], (count,) + v.shape), axes, 0, 0)


def copies_kernel(late_ref, v_ref, out_ref):
    del late_ref
    for i in range(out_ref.shape[0]):
        out_ref[i] = v_ref[...]


def spread_z(v, late):
    copies = pl.pallas_call(
        copies_kernel,
        out_shape=jax.ShapeDtypeStruct((NZ,) + v.shape, v.dtype),
        in_specs=[ANY, WHOLE],
        out_specs=WHOLE,
        compiler_params=pltpu.CompilerParams(vmem_limit_bytes=VMEM_LIMIT),
    )(late, v)
    return lax.all_to_all(copies, Z, 0, 0)


def cut_kernel(at_ref, acts_ref, grads_ref, own_ref, after_ref, before_ref, across_ref):
    y, core = at_ref[0], at_ref[1]
    width = own_ref.shape[3] // 2
    for z in range(2):
        for steps, out in ((0, own_ref), (1, after_ref), (3, before_ref), (2, across_ref)):
            block = z * NY + lax.rem(y + steps, NY)
            cols = pl.ds(pl.multiple_of(block * width, width), width)
            for i, values in enumerate((acts_ref, grads_ref)):
                if steps == 0:
                    out[i, :, :, z * width : (z + 1) * width] = values[:, :, cols]
                else:
                    out[i, :, z * width : (z + 1) * width] = values[core, :, cols]


def cut_features(at, acts, grads):
    seqs, tokens, features = acts.shape
    steps = NZ // 2
    part = features // NY // steps
    whole_spec = pl.BlockSpec((seqs, tokens, part * NY), lambda i: (0, 0, i))
    piece = jax.ShapeDtypeStruct((2, tokens, features // NY), acts.dtype)
    piece_spec = pl.BlockSpec((2, tokens, part), lambda i: (0, 0, i))
    return pl.pallas_call(
        cut_kernel,
        grid=(steps,),
        out_shape=(
            jax.ShapeDtypeStruct((2, seqs, tokens, features // NY), acts.dtype),
            piece,
            piece,
            piece,
        ),
        in_specs=[SCALARS, whole_spec, whole_spec],
        out_specs=(pl.BlockSpec((2, seqs, tokens, part), lambda i: (0, 0, 0, i)),)
        + (piece_spec,) * 3,
        compiler_params=pltpu.CompilerParams(vmem_limit_bytes=VMEM_LIMIT),
    )(at, acts, grads)


def turn_kernel(at_ref, own_ref, *refs):
    pieces, bases, (send_ref, full_ref, rows) = refs[:6], refs[6:8], refs[8:11]
    basis_rows, sems = refs[11], refs[12]
    y, core = at_ref[0], at_ref[1]
    tokens = own_ref.shape[2]
    copies = [pltpu.make_async_copy(own_ref, rows.at[:, 0:2], sems.at[0])]
    for i, piece in enumerate(pieces):
        copies.append(pltpu.make_async_copy(piece, rows.at[:, 2 + i], sems.at[1 + i]))
    copies += [
        pltpu.make_async_copy(bases[i], basis_rows[i], sems.at[7 + i]) for i in range(2)
    ]
    for copy in copies:
        copy.start()
    for copy in copies[:-2]:
        copy.wait()
    places = [(0, y), (1, y)]
    for seq in (core, 1 - core):
        places += [(seq, lax.rem(y + steps, NY)) for steps in (3, 1, 2)]
    act_cols, cols = bases[0].shape[1], full_ref.shape[3]
    for which, span in ((0, slice(0, act_cols)), (1, slice(act_cols, cols))):
        copies[which - 2].wait()
        product = jnp.dot(
            rows[which].reshape(8 * tokens, rows.shape[3]),
            basis_rows[which][...],
            preferred_element_type=jnp.float32,
        )
        rounded = product.astype(send_ref.dtype)
        rest = (product - rounded.astype(jnp.float32)).astype(send_ref.dtype)
        for i, (seq, source) in enumerate(places):
            part = slice(i * tokens, (i + 1) * tokens)
            full_ref[seq, source, :, span] = product[part]
            send_ref[seq, source, :, span] = rounded[part]
            if which == 1:
                send_ref[seq, source, :, cols:] = rest[part]


def turn(at, own, pieces, act_rows, grad_rows):
    _, seqs, tokens, features = own.shape
    act_cols, grad_cols = act_rows.shape[1], grad_rows.shape[1]
    cols = act_cols + grad_cols
    send, full = pl.pallas_call(
        turn_kernel,
        out_shape=(
            jax.ShapeDtypeStruct((seqs, NY, tokens, cols + grad_cols), jnp.bfloat16),
            jax.ShapeDtypeStruct((seqs, NY, tokens, cols), jnp.float32),
        ),
        in_specs=[SCALARS] + [IN_HBM] * (3 + len(pieces)),
        out_specs=(WHOLE, WHOLE),
        scratch_shapes=[
            pltpu.VMEM((2, 8, tokens, features), own.dtype),
            [pltpu.VMEM(act_rows.shape, own.dtype), pltpu.VMEM(grad_rows.shape, own.dtype)],
            pltpu.SemaphoreType.DMA((9,)),
        ],
        compiler_params=pltpu.CompilerParams(vmem_limit_bytes=TURN_LIMIT),
    )(at, own, *pieces, act_rows, grad_rows)
    return send.reshape(NY, -1, cols + grad_cols), full.reshape(NY, -1, cols)


def sum_kernel(at_ref, full_ref, got_ref, act_ref, grad_ref):
    y = at_ref[0]
    act_cols, cols = act_ref.shape[1], full_ref.shape[2]
    total = full_ref[y]
    acts, grads = total[:, :act_cols], total[:, act_cols:]
    for steps in range(1, NY):
        got = got_ref[lax.rem(y + steps, NY)].astype(jnp.float32)
        acts = acts + got[:, :act_cols]
        grads = grads + (got[:, act_cols:cols] + got[:, cols:])
    act_ref[...] = acts.astype(act_ref.dtype)
    grads = grads.astype(grad_ref.dtype)
    for i in range(NZ):
        grad_ref[i] = grads


def sum_parts(at, full, got, act_cols):
    rows, grad_cols = full.shape[1], full.shape[2] - act_cols
    return pl.pallas_call(
        sum_kernel,
        out_shape=(
            jax.ShapeDtypeStruct((rows, act_cols), jnp.bfloat16),
            jax.ShapeDtypeStruct((NZ, rows, grad_cols), jnp.bfloat16),
        ),
        in_specs=[SCALARS, WHOLE, WHOLE],
        out_specs=(WHOLE, WHOLE),
        compiler_params=pltpu.CompilerParams(vmem_limit_bytes=VMEM_LIMIT),
    )(at, full, got)


def outer_kernel(acts_ref, mine_ref, other_ref, keep_ref, send_ref):
    for grads_ref, out_ref in ((other_ref, send_ref), (mine_ref, keep_ref)):
        product = lax.dot_general(
            acts_ref[...],
            grads_ref[...],
            (((0,), (0,)), ((), ())),
            preferred_element_type=jnp.float32,
        )
        out_ref[...] = product.astype(out_ref.dtype)


def outer_product(at, acts, mine, other):
    out = jax.ShapeDtypeStruct((acts.shape[1], mine.shape[1]), jnp.bfloat16)
    keep, send = pl.pallas_call(
        outer_kernel,
        out_shape=(out, out),
        in_specs=[WHOLE] * 3,
        out_specs=(WHOLE, WHOLE),
        compiler_params=pltpu.CompilerParams(vmem_limit_bytes=VMEM_LIMIT),
    )(acts, mine, other)
    got = swap_cores(send)
    core = at[1]
    halves = jnp.stack([jnp.where(core == 0, keep, got), jnp.where(core == 0, got, keep)])
    return halves.reshape(NY, -1, keep.shape[1])


def local(activations, out_grads, act_basis, grad_basis):
    h = lax.axis_index(H)
    at = jnp.stack([lax.axis_index(Y), lax.axis_index(C)]).astype(jnp.int32)
    act_cols, grad_cols = act_basis.shape[1], grad_basis.shape[1]
    act_rows = lax.all_gather(act_basis, Z, axis=0, tiled=True)

    own, to_after, to_before, to_across = cut_features(at, activations, out_grads)
    pieces = [
        ring_y(to_after, one_way(1)),
        ring_y(to_before, one_way(-1)),
        ring_y(to_across, either_way),
    ]
    grad_rows = spread_z(grad_basis, at).reshape(-1, grad_cols)
    pieces += [swap_cores(v) for v in pieces]

    send, full = turn(at, own, pieces, act_rows, grad_rows)
    got = lax.all_to_all(send, Y, 0, 0)
    act_turned, grad_turned = sum_parts(at, full, got, act_cols)

    grad_panel = lax.all_to_all(grad_turned, Z, 0, 0).reshape(-1, grad_cols)
    near, far = transpose_planes(act_turned, 0), transpose_planes(act_turned, 1)
    pair = jnp.where(h == 0, jnp.stack([near, far]), jnp.stack([far, near]))
    act_panel = spread(pair, X, NX).reshape(-1, act_cols)

    outer = outer_product(at, act_panel, grad_panel, swap_cores(grad_panel))
    got = lax.all_to_all(outer, Y, 0, 0).astype(jnp.float32)
    first, second = got[0] + got[1], got[2] + got[3]
    count = activations.shape[0] * activations.shape[1] * NZ * NY
    return ((first * first + second * second) / count).T


def solution(mesh):
    fine = Mesh(mesh.devices.reshape(NZ, NY, NX, NH, NC), (Z, Y, X, H, C))
    dp, tensor = (Z, Y), (X, H, C)
    placed = (P(None, dp, None), P(None, dp, None), P(dp, tensor), P(dp, tensor))
    return jax.shard_map(
        local, mesh=fine, in_specs=placed, out_specs=P(tensor, dp), check_vma=False
    )
```

```python
import jax
import jax.numpy as jnp
from jax import lax
from jax.experimental import pallas as pl
from jax.experimental.pallas import tpu as pltpu
from jax.sharding import Mesh, PartitionSpec as P

Z, Y, X, H, C = "z", "y", "x", "h", "c"
NZ, NY, NX, NH, NC = 8, 4, 4, 2, 2

VMEM_LIMIT = 12 * 2**20
TURN_LIMIT = 60 * 2**20
SCALARS = pl.BlockSpec(memory_space=pltpu.SMEM)
WHOLE = pl.BlockSpec(memory_space=pltpu.VMEM)
IN_HBM = pl.BlockSpec(memory_space=pltpu.HBM)
ANY = pl.BlockSpec(memory_space=pl.ANY)


def swap_cores(v):
    return lax.ppermute(v, C, [(0, 1), (1, 0)])


def ring_y(v, shift):
    pairs = []
    for at in range(NH * NY):
        to = (at + shift(at)) % (NH * NY)
        pairs.append((at % NY * NH + at // NY, to % NY * NH + to // NY))
    return lax.ppermute(v, (Y, H), pairs)


def one_way(step):
    return lambda at: step


def either_way(at):
    return 2 if at % 2 == 0 else -2


def transpose_planes(v, flip):
    pairs = []
    for z in range(NZ):
        for t in range(NX * NH):
            pairs.append((z * NX * NH + t, t * NX * NH + (z ^ flip)))
    return lax.ppermute(v, (Z, X, H), pairs)


def copies_kernel(late_ref, v_ref, out_ref):
    del late_ref
    for i in range(out_ref.shape[0]):
        out_ref[i] = v_ref[...]


def spread_z(v, late):
    copies = pl.pallas_call(
        copies_kernel,
        out_shape=jax.ShapeDtypeStruct((NZ,) + v.shape, v.dtype),
        in_specs=[ANY, WHOLE],
        out_specs=WHOLE,
        compiler_params=pltpu.CompilerParams(vmem_limit_bytes=VMEM_LIMIT),
    )(late, v)
    return lax.all_to_all(copies, Z, 0, 0)


def cut_kernel(at_ref, values_ref, own_ref, after_ref, before_ref, across_ref):
    y, core = at_ref[0], at_ref[1]
    width = own_ref.shape[2] // 2
    for z in range(2):
        out_cols = slice(z * width, (z + 1) * width)
        for steps, out in ((0, own_ref), (1, after_ref), (3, before_ref), (2, across_ref)):
            block = z * NY + lax.rem(y + steps, NY)
            cols = pl.ds(pl.multiple_of(block * width, width), width)
            if steps == 0:
                out[:, :, out_cols] = values_ref[:, :, cols]
            else:
                out[:, out_cols] = values_ref[core, :, cols]


def cut_features(at, values):
    seqs, tokens, features = values.shape
    steps = NZ // 2
    part = features // NY // steps
    piece = jax.ShapeDtypeStruct((tokens, features // NY), values.dtype)
    piece_spec = pl.BlockSpec((tokens, part), lambda i: (0, i))
    return pl.pallas_call(
        cut_kernel,
        grid=(steps,),
        out_shape=(
            jax.ShapeDtypeStruct((seqs, tokens, features // NY), values.dtype),
            piece,
            piece,
            piece,
        ),
        in_specs=[SCALARS, pl.BlockSpec((seqs, tokens, part * NY), lambda i: (0, 0, i))],
        out_specs=(pl.BlockSpec((seqs, tokens, part), lambda i: (0, 0, i)),) + (piece_spec,) * 3,
        compiler_params=pltpu.CompilerParams(vmem_limit_bytes=VMEM_LIMIT),
    )(at, values)


def move_tokens(at, values):
    own, to_after, to_before, to_across = cut_features(at, values)
    pieces = [
        ring_y(to_after, one_way(1)),
        ring_y(to_before, one_way(-1)),
        ring_y(to_across, either_way),
    ]
    return own, pieces


def turn_kernel(lates, at_ref, *refs):
    own_ref, *pieces, basis_ref, out_ref, rows, basis, sems = refs[lates:]
    y, core = at_ref[0], at_ref[1]
    tokens = own_ref.shape[1]
    copies = [
        pltpu.make_async_copy(own_ref, rows.at[0:2], sems.at[0]),
        pltpu.make_async_copy(basis_ref, basis, sems.at[1]),
    ]
    for i, piece in enumerate(pieces):
        copies.append(pltpu.make_async_copy(piece, rows.at[2 + i], sems.at[2 + i]))
    for copy in copies:
        copy.start()
    for copy in copies:
        copy.wait()
    product = jnp.dot(
        rows[...].reshape(8 * tokens, rows.shape[2]),
        basis[...],
        preferred_element_type=jnp.float32,
    )
    parts = out_ref.shape[2]
    if parts == 1:
        columns = [product]
    else:
        half = out_ref.shape[5] // 2
        columns = []
        for c in range(parts):
            halves = [
                product[:, (parts * q + c) * half : (parts * q + c + 1) * half]
                for q in range(2)
            ]
            columns.append(jnp.concatenate(halves, axis=1))
    places = [(0, y), (1, y)]
    for seq in (core, 1 - core):
        places += [(seq, lax.rem(y + steps, NY)) for steps in (3, 1, 2)]
    for i, (seq, source) in enumerate(places):
        for c in range(parts):
            out_ref[seq, source // 2, c, lax.rem(source, 2)] = columns[c][
                i * tokens : (i + 1) * tokens
            ]


def turn(at, late, own, pieces, basis, parts):
    seqs, tokens, features = own.shape
    cols = basis.shape[1]
    out = pl.pallas_call(
        lambda *refs: turn_kernel(len(late), *refs),
        out_shape=jax.ShapeDtypeStruct(
            (seqs, 2, parts, 2, tokens, cols // parts), jnp.float32
        ),
        in_specs=[SCALARS] + [ANY] * (2 + len(late) + len(pieces)),
        out_specs=WHOLE,
        scratch_shapes=[
            pltpu.VMEM((8, tokens, features), own.dtype),
            pltpu.VMEM((features, cols), basis.dtype),
            pltpu.SemaphoreType.DMA((8,)),
        ],
        compiler_params=pltpu.CompilerParams(vmem_limit_bytes=TURN_LIMIT),
    )(at, *late, own, *pieces, basis)
    return out.reshape(NY * parts, 2 * tokens, cols // parts)


def round_kernel(late_ref, v_ref, out_ref):
    del late_ref
    out_ref[...] = v_ref[...].astype(out_ref.dtype)


def rounded(late, v):
    return pl.pallas_call(
        round_kernel,
        out_shape=jax.ShapeDtypeStruct(v.shape, jnp.bfloat16),
        in_specs=[ANY, WHOLE],
        out_specs=WHOLE,
        compiler_params=pltpu.CompilerParams(vmem_limit_bytes=VMEM_LIMIT),
    )(late, v)


def sum_acts_kernel(at_ref, full_ref, got_ref, out_ref):
    y, core = at_ref[0], at_ref[1]
    totals = []
    for c in range(NC):
        own = NC * y + c
        total = jnp.where(core == c, full_ref[own], got_ref[own].astype(jnp.float32))
        for steps in range(1, NY):
            source = NC * lax.rem(y + steps, NY) + c
            total = total + got_ref[source].astype(jnp.float32)
        totals.append(total)
    out_ref[...] = jnp.concatenate(totals, axis=1).astype(out_ref.dtype)


def sum_acts(at, full, got):
    _, rows, cols = full.shape
    return pl.pallas_call(
        sum_acts_kernel,
        out_shape=jax.ShapeDtypeStruct((rows, NC * cols), jnp.bfloat16),
        in_specs=[SCALARS, WHOLE, WHOLE],
        out_specs=WHOLE,
        compiler_params=pltpu.CompilerParams(vmem_limit_bytes=VMEM_LIMIT),
    )(at, full, got)


def sum_grads_kernel(late_ref, got_ref, out_ref):
    del late_ref
    total = got_ref[0] + got_ref[1] + got_ref[2] + got_ref[3]
    out_ref[...] = total


def sum_grads(late, got):
    return pl.pallas_call(
        sum_grads_kernel,
        out_shape=jax.ShapeDtypeStruct(got.shape[1:], got.dtype),
        in_specs=[ANY, WHOLE],
        out_specs=WHOLE,
        compiler_params=pltpu.CompilerParams(vmem_limit_bytes=VMEM_LIMIT),
    )(late, got)


def pair_kernel(at_ref, near_ref, far_ref, out_ref):
    even = at_ref[2] == 0
    near, far = near_ref[...], far_ref[...]
    first, second = jnp.where(even, near, far), jnp.where(even, far, near)
    for i in range(NX):
        out_ref[i, 0] = first
        out_ref[i, 1] = second


def paired(at, near, far):
    return pl.pallas_call(
        pair_kernel,
        out_shape=jax.ShapeDtypeStruct((NX, 2) + near.shape, near.dtype),
        in_specs=[SCALARS, WHOLE, WHOLE],
        out_specs=WHOLE,
        compiler_params=pltpu.CompilerParams(vmem_limit_bytes=VMEM_LIMIT),
    )(at, near, far)


def outer_kernel(at_ref, acts_ref, mine_ref, other_ref, out_ref):
    core = at_ref[1]
    quarter = out_ref.shape[2]
    for grads_ref, place in ((mine_ref, core), (other_ref, 1 - core)):
        product = lax.dot_general(
            acts_ref[...],
            grads_ref[...].astype(acts_ref.dtype),
            (((0,), (0,)), ((), ())),
            preferred_element_type=jnp.float32,
        ).astype(out_ref.dtype)
        for q in range(NY):
            out_ref[q, place] = product[q * quarter : (q + 1) * quarter]


def outer_product(at, acts, mine, other):
    quarter, cols = acts.shape[1] // NY, mine.shape[1]
    out = pl.pallas_call(
        outer_kernel,
        out_shape=jax.ShapeDtypeStruct((NY, NC, quarter, cols), jnp.bfloat16),
        in_specs=[SCALARS] + [WHOLE] * 3,
        out_specs=WHOLE,
        compiler_params=pltpu.CompilerParams(vmem_limit_bytes=VMEM_LIMIT),
    )(at, acts, mine, other)
    return out.reshape(NY * NC, quarter, cols)


def local(activations, out_grads, act_basis, grad_basis):
    at = jnp.stack([lax.axis_index(a) for a in (Y, C, H)]).astype(jnp.int32)
    act_cols, grad_cols = act_basis.shape[1], grad_basis.shape[1]
    act_rows = lax.all_gather(act_basis, Z, axis=0, tiled=True)

    grad_rows = spread_z(grad_basis, at).reshape(-1, grad_cols)
    grad_own, grad_pieces = move_tokens(at, out_grads)
    act_own, act_pieces = move_tokens(at, activations)
    grad_pieces = grad_pieces + [swap_cores(v) for v in grad_pieces]

    grad_part = turn(at, act_pieces, grad_own, grad_pieces, grad_rows, 1)
    grad_got = lax.all_to_all(grad_part, Y, 0, 0)
    act_pieces = act_pieces + [swap_cores(v) for v in act_pieces]
    act_part = turn(at, [grad_part], act_own, act_pieces, act_rows, NC)
    act_got = lax.all_to_all(rounded(at, act_part), (Y, C), 0, 0)

    grad_turned = sum_grads(act_part, grad_got)
    grad_panel = lax.all_gather(grad_turned, Z, axis=0, tiled=True)

    act_turned = sum_acts(at, act_part, act_got)
    near, far = transpose_planes(act_turned, 0), transpose_planes(act_turned, 1)
    pair = paired(at, near, far)
    act_panel = lax.all_to_all(pair, X, 0, 0).reshape(-1, act_cols)
    grad_panel = rounded(pair, grad_panel)

    outer = outer_product(at, act_panel, grad_panel, swap_cores(grad_panel))
    got = lax.all_to_all(outer, (Y, C), 0, 0).astype(jnp.float32)
    got = got.reshape(NY, -1, got.shape[2])
    first, second = got[0] + got[1], got[2] + got[3]
    count = activations.shape[0] * activations.shape[1] * NZ * NY
    return ((first * first + second * second) / count).T


def solution(mesh):
    fine = Mesh(mesh.devices.reshape(NZ, NY, NX, NH, NC), (Z, Y, X, H, C))
    dp, tensor = (Z, Y), (X, H, C)
    placed = (P(None, dp, None), P(None, dp, None), P(dp, tensor), P(dp, tensor))
    return jax.shard_map(
        local, mesh=fine, in_specs=placed, out_specs=P(tensor, dp), check_vma=False
    )
```

```python
import jax
import jax.numpy as jnp
from jax import lax
from jax.experimental import pallas as pl
from jax.experimental.pallas import tpu as pltpu
from jax.sharding import Mesh, PartitionSpec as P

Z, Y, X, H, C = "z", "y", "x", "h", "c"
NZ, NY, NX, NH, NC = 8, 4, 4, 2, 2

VMEM_LIMIT = 12 * 2**20
TURN_LIMIT = 60 * 2**20
SCALARS = pl.BlockSpec(memory_space=pltpu.SMEM)
WHOLE = pl.BlockSpec(memory_space=pltpu.VMEM)
IN_HBM = pl.BlockSpec(memory_space=pltpu.HBM)
ANY = pl.BlockSpec(memory_space=pl.ANY)


def swap_cores(v):
    return lax.ppermute(v, C, [(0, 1), (1, 0)])


def permute(v, axes, sizes, move):
    count = 1
    for size in sizes:
        count *= size
    pairs = []
    for at in range(count):
        place, rest = [], at
        for size in reversed(sizes):
            place.insert(0, rest % size)
            rest //= size
        to = 0
        for index, size in zip(move(*place), sizes):
            to = to * size + index
        pairs.append((at, to))
    return lax.ppermute(v, axes, pairs)


def on_ring(y, h, steps):
    at = (h * NY + y + steps) % (NH * NY)
    return at % NY, at // NY


def to_neighbours(v):
    return permute(
        v, (Y, H, C), (NY, NH, NC), lambda y, h, c: (*on_ring(y, h, 1 - 2 * c), c)
    )


def to_across(v):
    return permute(
        v, (Y, H), (NY, NH), lambda y, h: on_ring(y, h, 2 if y % 2 == 0 else -2)
    )


def transpose_planes(v, flip):
    pairs = []
    for z in range(NZ):
        for t in range(NX * NH):
            pairs.append((z * NX * NH + t, t * NX * NH + (z ^ flip)))
    return lax.ppermute(v, (Z, X, H), pairs)


def copies_kernel(late_ref, v_ref, out_ref):
    del late_ref
    for i in range(out_ref.shape[0]):
        out_ref[i] = v_ref[...]


def spread_z(v, late):
    copies = pl.pallas_call(
        copies_kernel,
        out_shape=jax.ShapeDtypeStruct((NZ,) + v.shape, v.dtype),
        in_specs=[ANY, WHOLE],
        out_specs=WHOLE,
        compiler_params=pltpu.CompilerParams(vmem_limit_bytes=VMEM_LIMIT),
    )(late, v)
    return lax.all_to_all(copies, Z, 0, 0)


def cut_kernel(at_ref, values_ref, own_ref, near_ref, across_ref):
    y, core = at_ref[0], at_ref[1]
    width = own_ref.shape[2] // 2
    for z in range(2):
        out = slice(z * width, (z + 1) * width)
        for steps, out_ref in ((0, own_ref), (1 + 2 * core, near_ref), (2, across_ref)):
            block = z * NY + lax.rem(y + steps, NY)
            cols = pl.ds(pl.multiple_of(block * width, width), width)
            if out_ref is across_ref:
                out_ref[:, out] = values_ref[core, :, cols]
            else:
                out_ref[:, :, out] = values_ref[:, :, cols]


def cut_features(at, values):
    seqs, tokens, features = values.shape
    steps = NZ // 2
    part = features // NY // steps
    both = jax.ShapeDtypeStruct((seqs, tokens, features // NY), values.dtype)
    both_spec = pl.BlockSpec((seqs, tokens, part), lambda i: (0, 0, i))
    return pl.pallas_call(
        cut_kernel,
        grid=(steps,),
        out_shape=(both, both, jax.ShapeDtypeStruct((tokens, features // NY), values.dtype)),
        in_specs=[SCALARS, pl.BlockSpec((seqs, tokens, part * NY), lambda i: (0, 0, i))],
        out_specs=(both_spec, both_spec, pl.BlockSpec((tokens, part), lambda i: (0, i))),
        compiler_params=pltpu.CompilerParams(vmem_limit_bytes=VMEM_LIMIT),
    )(at, values)


def move_tokens(at, values):
    own, near, across = cut_features(at, values)
    return own, [to_neighbours(near), to_across(across)]


def turn_kernel(lates, at_ref, *refs):
    own_ref, near, across, near_other, across_other, basis_ref = refs[lates : lates + 6]
    *outs, rows, basis, sems = refs[lates + 6 :]
    y, core = at_ref[0], at_ref[1]
    tokens = own_ref.shape[1]
    copies = [
        pltpu.make_async_copy(own_ref, rows.at[0:2], sems.at[0]),
        pltpu.make_async_copy(near, rows.at[2:4], sems.at[1]),
        pltpu.make_async_copy(near_other, rows.at[4:6], sems.at[2]),
        pltpu.make_async_copy(across, rows.at[6], sems.at[3]),
        pltpu.make_async_copy(across_other, rows.at[7], sems.at[4]),
        pltpu.make_async_copy(basis_ref, basis, sems.at[5]),
    ]
    for copy in copies:
        copy.start()
    for copy in copies:
        copy.wait()
    product = jnp.dot(
        rows[...].reshape(8 * tokens, rows.shape[2]),
        basis[...],
        preferred_element_type=jnp.float32,
    )
    parts = outs[0].shape[2]
    if parts == 1:
        columns = [product]
    else:
        half = outs[0].shape[5] // 2
        columns = []
        for c in range(parts):
            halves = [
                product[:, (parts * q + c) * half : (parts * q + c + 1) * half]
                for q in range(2)
            ]
            columns.append(jnp.concatenate(halves, axis=1))
    back, on = lax.rem(y + 3 - 2 * core, NY), lax.rem(y + 1 + 2 * core, NY)
    two = lax.rem(y + 2, NY)
    places = [(0, y), (1, y), (0, back), (1, back), (0, on), (1, on), (core, two), (1 - core, two)]
    for i, (seq, source) in enumerate(places):
        for c in range(parts):
            value = columns[c][i * tokens : (i + 1) * tokens]
            for out_ref in outs:
                out_ref[seq, source // 2, c, lax.rem(source, 2)] = value.astype(out_ref.dtype)


def turn(at, late, own, pieces, basis, parts, dtypes):
    seqs, tokens, features = own.shape
    cols = basis.shape[1]
    shape = (seqs, 2, parts, 2, tokens, cols // parts)
    outs = pl.pallas_call(
        lambda *refs: turn_kernel(len(late), *refs),
        out_shape=tuple(jax.ShapeDtypeStruct(shape, dtype) for dtype in dtypes),
        in_specs=[SCALARS] + [ANY] * (2 + len(late) + len(pieces)),
        out_specs=(WHOLE,) * len(dtypes),
        scratch_shapes=[
            pltpu.VMEM((8, tokens, features), own.dtype),
            pltpu.VMEM((features, cols), basis.dtype),
            pltpu.SemaphoreType.DMA((6,)),
        ],
        compiler_params=pltpu.CompilerParams(vmem_limit_bytes=TURN_LIMIT),
    )(at, *late, own, *pieces, basis)
    return [out.reshape(NY * parts, 2 * tokens, cols // parts) for out in outs]


def round_kernel(late_ref, v_ref, out_ref):
    del late_ref
    out_ref[...] = v_ref[...].astype(out_ref.dtype)


def rounded(late, v):
    return pl.pallas_call(
        round_kernel,
        out_shape=jax.ShapeDtypeStruct(v.shape, jnp.bfloat16),
        in_specs=[ANY, WHOLE],
        out_specs=WHOLE,
        compiler_params=pltpu.CompilerParams(vmem_limit_bytes=VMEM_LIMIT),
    )(late, v)


def sum_acts_kernel(at_ref, full_ref, got_ref, out_ref):
    y, core = at_ref[0], at_ref[1]
    totals = []
    for c in range(NC):
        own = NC * y + c
        total = jnp.where(core == c, full_ref[own], got_ref[own].astype(jnp.float32))
        for steps in range(1, NY):
            source = NC * lax.rem(y + steps, NY) + c
            total = total + got_ref[source].astype(jnp.float32)
        totals.append(total)
    out_ref[...] = jnp.concatenate(totals, axis=1).astype(out_ref.dtype)


def sum_acts(at, full, got):
    _, rows, cols = full.shape
    return pl.pallas_call(
        sum_acts_kernel,
        out_shape=jax.ShapeDtypeStruct((rows, NC * cols), jnp.bfloat16),
        in_specs=[SCALARS, WHOLE, WHOLE],
        out_specs=WHOLE,
        compiler_params=pltpu.CompilerParams(vmem_limit_bytes=VMEM_LIMIT),
    )(at, full, got)


def sum_grads_kernel(late_ref, got_ref, out_ref):
    del late_ref
    total = got_ref[0] + got_ref[1] + got_ref[2] + got_ref[3]
    out_ref[...] = total


def sum_grads(late, got):
    return pl.pallas_call(
        sum_grads_kernel,
        out_shape=jax.ShapeDtypeStruct(got.shape[1:], got.dtype),
        in_specs=[ANY, WHOLE],
        out_specs=WHOLE,
        compiler_params=pltpu.CompilerParams(vmem_limit_bytes=VMEM_LIMIT),
    )(late, got)


def pair_kernel(at_ref, near_ref, far_ref, out_ref):
    even = at_ref[2] == 0
    near, far = near_ref[...], far_ref[...]
    first, second = jnp.where(even, near, far), jnp.where(even, far, near)
    for i in range(NX):
        out_ref[i, 0] = first
        out_ref[i, 1] = second


def paired(at, near, far):
    return pl.pallas_call(
        pair_kernel,
        out_shape=jax.ShapeDtypeStruct((NX, 2) + near.shape, near.dtype),
        in_specs=[SCALARS, WHOLE, WHOLE],
        out_specs=WHOLE,
        compiler_params=pltpu.CompilerParams(vmem_limit_bytes=VMEM_LIMIT),
    )(at, near, far)


def outer_kernel(at_ref, acts_ref, mine_ref, other_ref, out_ref):
    core = at_ref[1]
    quarter = out_ref.shape[2]
    for grads_ref, place in ((mine_ref, core), (other_ref, 1 - core)):
        product = lax.dot_general(
            acts_ref[...],
            grads_ref[...].astype(acts_ref.dtype),
            (((0,), (0,)), ((), ())),
            preferred_element_type=jnp.float32,
        ).astype(out_ref.dtype)
        for q in range(NY):
            out_ref[q, place] = product[q * quarter : (q + 1) * quarter]


def outer_product(at, acts, mine, other):
    quarter, cols = acts.shape[1] // NY, mine.shape[1]
    out = pl.pallas_call(
        outer_kernel,
        out_shape=jax.ShapeDtypeStruct((NY, NC, quarter, cols), jnp.bfloat16),
        in_specs=[SCALARS] + [WHOLE] * 3,
        out_specs=WHOLE,
        compiler_params=pltpu.CompilerParams(vmem_limit_bytes=VMEM_LIMIT),
    )(at, acts, mine, other)
    return out.reshape(NY * NC, quarter, cols)


def local(activations, out_grads, act_basis, grad_basis):
    at = jnp.stack([lax.axis_index(a) for a in (Y, C, H)]).astype(jnp.int32)
    act_cols, grad_cols = act_basis.shape[1], grad_basis.shape[1]
    act_rows = lax.all_gather(act_basis, Z, axis=0, tiled=True)

    grad_rows = spread_z(grad_basis, at).reshape(-1, grad_cols)
    grad_own, grad_pieces = move_tokens(at, out_grads)
    act_own, act_pieces = move_tokens(at, activations)
    grad_pieces = grad_pieces + [swap_cores(v) for v in grad_pieces]

    (grad_part,) = turn(at, act_pieces, grad_own, grad_pieces, grad_rows, 1, [jnp.float32])
    grad_got = lax.all_to_all(grad_part, Y, 0, 0)
    act_pieces = act_pieces + [swap_cores(v) for v in act_pieces]
    act_part, act_send = turn(
        at, [grad_part], act_own, act_pieces, act_rows, NC, [jnp.float32, jnp.bfloat16]
    )
    act_got = lax.all_to_all(act_send, (Y, C), 0, 0)

    grad_turned = sum_grads(act_part, grad_got)
    grad_panel = lax.all_gather(grad_turned, Z, axis=0, tiled=True)

    act_turned = sum_acts(at, act_part, act_got)
    near, far = transpose_planes(act_turned, 0), transpose_planes(act_turned, 1)
    pair = paired(at, near, far)
    act_panel = lax.all_to_all(pair, X, 0, 0).reshape(-1, act_cols)
    grad_panel = rounded(pair, grad_panel)

    outer = outer_product(at, act_panel, grad_panel, swap_cores(grad_panel))
    got = lax.all_to_all(outer, (Y, C), 0, 0).astype(jnp.float32)
    got = got.reshape(NY, -1, got.shape[2])
    first, second = got[0] + got[1], got[2] + got[3]
    count = activations.shape[0] * activations.shape[1] * NZ * NY
    return ((first * first + second * second) / count).T


def solution(mesh):
    fine = Mesh(mesh.devices.reshape(NZ, NY, NX, NH, NC), (Z, Y, X, H, C))
    dp, tensor = (Z, Y), (X, H, C)
    placed = (P(None, dp, None), P(None, dp, None), P(dp, tensor), P(dp, tensor))
    return jax.shard_map(
        local, mesh=fine, in_specs=placed, out_specs=P(tensor, dp), check_vma=False
    )
```

```python
import jax
import jax.numpy as jnp
from jax import lax
from jax.experimental import pallas as pl
from jax.experimental.pallas import tpu as pltpu
from jax.sharding import Mesh, PartitionSpec as P

Z, Y, X, H, C = "z", "y", "x", "h", "c"
NZ, NY, NX, NH, NC = 8, 4, 4, 2, 2

VMEM_LIMIT = 12 * 2**20
TURN_LIMIT = 60 * 2**20
SCALARS = pl.BlockSpec(memory_space=pltpu.SMEM)
WHOLE = pl.BlockSpec(memory_space=pltpu.VMEM)
IN_HBM = pl.BlockSpec(memory_space=pltpu.HBM)
ANY = pl.BlockSpec(memory_space=pl.ANY)


def swap_cores(v):
    return lax.ppermute(v, C, [(0, 1), (1, 0)])


def permute(v, axes, sizes, move):
    count = 1
    for size in sizes:
        count *= size
    pairs = []
    for at in range(count):
        place, rest = [], at
        for size in reversed(sizes):
            place.insert(0, rest % size)
            rest //= size
        to = 0
        for index, size in zip(move(*place), sizes):
            to = to * size + index
        pairs.append((at, to))
    return lax.ppermute(v, axes, pairs)


def on_ring(y, h, steps):
    at = (h * NY + y + steps) % (NH * NY)
    return at % NY, at // NY


def to_neighbours(v):
    return permute(
        v, (Y, H, C), (NY, NH, NC), lambda y, h, c: (*on_ring(y, h, 1 - 2 * c), c)
    )


def to_across(v):
    return permute(
        v, (Y, H), (NY, NH), lambda y, h: on_ring(y, h, 2 if y % 2 == 0 else -2)
    )


def transpose_planes(v, flip):
    pairs = []
    for z in range(NZ):
        for t in range(NX * NH):
            pairs.append((z * NX * NH + t, t * NX * NH + (z ^ flip)))
    return lax.ppermute(v, (Z, X, H), pairs)


def copies_kernel(late_ref, v_ref, out_ref):
    del late_ref
    for i in range(out_ref.shape[0]):
        out_ref[i] = v_ref[...]


def spread_z(v, late):
    copies = pl.pallas_call(
        copies_kernel,
        out_shape=jax.ShapeDtypeStruct((NZ,) + v.shape, v.dtype),
        in_specs=[ANY, WHOLE],
        out_specs=WHOLE,
        compiler_params=pltpu.CompilerParams(vmem_limit_bytes=VMEM_LIMIT),
    )(late, v)
    return lax.all_to_all(copies, Z, 0, 0)


def cut_kernel(at_ref, values_ref, own_ref, near_ref, across_ref):
    y, core = at_ref[0], at_ref[1]
    width = own_ref.shape[2] // 2
    for z in range(2):
        out = slice(z * width, (z + 1) * width)
        for steps, out_ref in ((0, own_ref), (1 + 2 * core, near_ref), (2, across_ref)):
            block = z * NY + lax.rem(y + steps, NY)
            cols = pl.ds(pl.multiple_of(block * width, width), width)
            if out_ref is across_ref:
                out_ref[:, out] = values_ref[core, :, cols]
            else:
                out_ref[:, :, out] = values_ref[:, :, cols]


def cut_features(at, values):
    seqs, tokens, features = values.shape
    steps = NZ // 2
    part = features // NY // steps
    both = jax.ShapeDtypeStruct((seqs, tokens, features // NY), values.dtype)
    both_spec = pl.BlockSpec((seqs, tokens, part), lambda i: (0, 0, i))
    return pl.pallas_call(
        cut_kernel,
        grid=(steps,),
        out_shape=(both, both, jax.ShapeDtypeStruct((tokens, features // NY), values.dtype)),
        in_specs=[SCALARS, pl.BlockSpec((seqs, tokens, part * NY), lambda i: (0, 0, i))],
        out_specs=(both_spec, both_spec, pl.BlockSpec((tokens, part), lambda i: (0, i))),
        compiler_params=pltpu.CompilerParams(vmem_limit_bytes=VMEM_LIMIT),
    )(at, values)


def move_tokens(at, values):
    own, near, across = cut_features(at, values)
    return own, [to_neighbours(near), to_across(across)]


def turn_kernel(lates, at_ref, *refs):
    own_ref, near, across, near_other, across_other, basis_ref = refs[lates : lates + 6]
    *outs, rows, basis, sems = refs[lates + 6 :]
    y, core = at_ref[0], at_ref[1]
    tokens = own_ref.shape[1]
    copies = [
        pltpu.make_async_copy(own_ref, rows.at[0:2], sems.at[0]),
        pltpu.make_async_copy(near, rows.at[2:4], sems.at[1]),
        pltpu.make_async_copy(near_other, rows.at[4:6], sems.at[2]),
        pltpu.make_async_copy(across, rows.at[6], sems.at[3]),
        pltpu.make_async_copy(across_other, rows.at[7], sems.at[4]),
        pltpu.make_async_copy(basis_ref, basis, sems.at[5]),
    ]
    for copy in copies:
        copy.start()
    for copy in copies:
        copy.wait()
    product = jnp.dot(
        rows[...].reshape(8 * tokens, rows.shape[2]),
        basis[...],
        preferred_element_type=jnp.float32,
    )
    parts = outs[0].shape[2]
    if parts == 1:
        columns = [product]
    else:
        half = outs[0].shape[5] // 2
        columns = []
        for c in range(parts):
            halves = [
                product[:, (parts * q + c) * half : (parts * q + c + 1) * half]
                for q in range(2)
            ]
            columns.append(jnp.concatenate(halves, axis=1))
    back, on = lax.rem(y + 3 - 2 * core, NY), lax.rem(y + 1 + 2 * core, NY)
    two = lax.rem(y + 2, NY)
    places = [(0, y), (1, y), (0, back), (1, back), (0, on), (1, on), (core, two), (1 - core, two)]
    for i, (seq, source) in enumerate(places):
        for c in range(parts):
            value = columns[c][i * tokens : (i + 1) * tokens]
            for out_ref in outs:
                out_ref[seq, source // 2, c, lax.rem(source, 2)] = value.astype(out_ref.dtype)


def turn(at, late, own, pieces, basis, parts, dtypes):
    seqs, tokens, features = own.shape
    cols = basis.shape[1]
    shape = (seqs, 2, parts, 2, tokens, cols // parts)
    outs = pl.pallas_call(
        lambda *refs: turn_kernel(len(late), *refs),
        out_shape=tuple(jax.ShapeDtypeStruct(shape, dtype) for dtype in dtypes),
        in_specs=[SCALARS] + [ANY] * (2 + len(late) + len(pieces)),
        out_specs=(WHOLE,) * len(dtypes),
        scratch_shapes=[
            pltpu.VMEM((8, tokens, features), own.dtype),
            pltpu.VMEM((features, cols), basis.dtype),
            pltpu.SemaphoreType.DMA((6,)),
        ],
        compiler_params=pltpu.CompilerParams(
            vmem_limit_bytes=TURN_LIMIT if parts > 1 else VMEM_LIMIT
        ),
    )(at, *late, own, *pieces, basis)
    return [out.reshape(NY * parts, 2 * tokens, cols // parts) for out in outs]


def round_kernel(late_ref, v_ref, out_ref):
    del late_ref
    out_ref[...] = v_ref[...].astype(out_ref.dtype)


def rounded(late, v):
    return pl.pallas_call(
        round_kernel,
        out_shape=jax.ShapeDtypeStruct(v.shape, jnp.bfloat16),
        in_specs=[ANY, WHOLE],
        out_specs=WHOLE,
        compiler_params=pltpu.CompilerParams(vmem_limit_bytes=VMEM_LIMIT),
    )(late, v)


def sum_acts_kernel(at_ref, full_ref, got_ref, out_ref):
    y, core = at_ref[0], at_ref[1]
    totals = []
    for c in range(NC):
        own = NC * y + c
        total = jnp.where(core == c, full_ref[own], got_ref[own].astype(jnp.float32))
        for steps in range(1, NY):
            source = NC * lax.rem(y + steps, NY) + c
            total = total + got_ref[source].astype(jnp.float32)
        totals.append(total)
    out_ref[...] = jnp.concatenate(totals, axis=1).astype(out_ref.dtype)


def sum_acts(at, full, got):
    _, rows, cols = full.shape
    return pl.pallas_call(
        sum_acts_kernel,
        out_shape=jax.ShapeDtypeStruct((rows, NC * cols), jnp.bfloat16),
        in_specs=[SCALARS, WHOLE, WHOLE],
        out_specs=WHOLE,
        compiler_params=pltpu.CompilerParams(vmem_limit_bytes=VMEM_LIMIT),
    )(at, full, got)


def sum_grads_kernel(late_ref, got_ref, out_ref):
    del late_ref
    total = got_ref[0] + got_ref[1] + got_ref[2] + got_ref[3]
    out_ref[...] = total


def sum_grads(late, got):
    return pl.pallas_call(
        sum_grads_kernel,
        out_shape=jax.ShapeDtypeStruct(got.shape[1:], got.dtype),
        in_specs=[ANY, WHOLE],
        out_specs=WHOLE,
        compiler_params=pltpu.CompilerParams(vmem_limit_bytes=VMEM_LIMIT),
    )(late, got)


def pair_kernel(at_ref, near_ref, far_ref, out_ref):
    even = at_ref[2] == 0
    near, far = near_ref[...], far_ref[...]
    first, second = jnp.where(even, near, far), jnp.where(even, far, near)
    for i in range(NX):
        out_ref[i, 0] = first
        out_ref[i, 1] = second


def paired(at, near, far):
    return pl.pallas_call(
        pair_kernel,
        out_shape=jax.ShapeDtypeStruct((NX, 2) + near.shape, near.dtype),
        in_specs=[SCALARS, WHOLE, WHOLE],
        out_specs=WHOLE,
        compiler_params=pltpu.CompilerParams(vmem_limit_bytes=VMEM_LIMIT),
    )(at, near, far)


def outer_kernel(at_ref, acts_ref, mine_ref, other_ref, out_ref):
    core = at_ref[1]
    quarter = out_ref.shape[2]
    for grads_ref, place in ((mine_ref, core), (other_ref, 1 - core)):
        product = lax.dot_general(
            acts_ref[...],
            grads_ref[...].astype(acts_ref.dtype),
            (((0,), (0,)), ((), ())),
            preferred_element_type=jnp.float32,
        ).astype(out_ref.dtype)
        for q in range(NY):
            out_ref[q, place] = product[q * quarter : (q + 1) * quarter]


def outer_product(at, acts, mine, other):
    quarter, cols = acts.shape[1] // NY, mine.shape[1]
    out = pl.pallas_call(
        outer_kernel,
        out_shape=jax.ShapeDtypeStruct((NY, NC, quarter, cols), jnp.bfloat16),
        in_specs=[SCALARS] + [WHOLE] * 3,
        out_specs=WHOLE,
        compiler_params=pltpu.CompilerParams(vmem_limit_bytes=VMEM_LIMIT),
    )(at, acts, mine, other)
    return out.reshape(NY * NC, quarter, cols)


def local(activations, out_grads, act_basis, grad_basis):
    at = jnp.stack([lax.axis_index(a) for a in (Y, C, H)]).astype(jnp.int32)
    act_cols, grad_cols = act_basis.shape[1], grad_basis.shape[1]
    act_rows = lax.all_gather(act_basis, Z, axis=0, tiled=True)

    grad_rows = spread_z(grad_basis, at).reshape(-1, grad_cols)
    grad_own, grad_pieces = move_tokens(at, out_grads)
    act_own, act_pieces = move_tokens(at, activations)
    grad_pieces = grad_pieces + [swap_cores(v) for v in grad_pieces]

    (grad_part,) = turn(at, act_pieces, grad_own, grad_pieces, grad_rows, 1, [jnp.float32])
    grad_got = lax.all_to_all(grad_part, Y, 0, 0)
    act_pieces = act_pieces + [swap_cores(v) for v in act_pieces]
    act_part, act_send = turn(
        at, [grad_part], act_own, act_pieces, act_rows, NC, [jnp.float32, jnp.bfloat16]
    )
    act_got = lax.all_to_all(act_send, (Y, C), 0, 0)

    grad_turned = sum_grads(act_part, grad_got)
    grad_panel = lax.all_gather(grad_turned, Z, axis=0, tiled=True)

    act_turned = sum_acts(at, act_part, act_got)
    near, far = transpose_planes(act_turned, 0), transpose_planes(act_turned, 1)
    pair = paired(at, near, far)
    act_panel = lax.all_to_all(pair, X, 0, 0).reshape(-1, act_cols)
    grad_panel = rounded(pair, grad_panel)

    outer = outer_product(at, act_panel, grad_panel, swap_cores(grad_panel))
    got = lax.all_to_all(outer, (Y, C), 0, 0).astype(jnp.float32)
    got = got.reshape(NY, -1, got.shape[2])
    first, second = got[0] + got[1], got[2] + got[3]
    count = activations.shape[0] * activations.shape[1] * NZ * NY
    return ((first * first + second * second) / count).T


def solution(mesh):
    fine = Mesh(mesh.devices.reshape(NZ, NY, NX, NH, NC), (Z, Y, X, H, C))
    dp, tensor = (Z, Y), (X, H, C)
    placed = (P(None, dp, None), P(None, dp, None), P(dp, tensor), P(dp, tensor))
    return jax.shard_map(
        local, mesh=fine, in_specs=placed, out_specs=P(tensor, dp), check_vma=False
    )
```

```python
import jax
import jax.numpy as jnp
from jax import lax
from jax.experimental import pallas as pl
from jax.experimental.pallas import tpu as pltpu
from jax.sharding import Mesh, PartitionSpec as P

Z, Y, X, H, C = "z", "y", "x", "h", "c"
NZ, NY, NX, NH, NC = 8, 4, 4, 2, 2

VMEM_LIMIT = 12 * 2**20
TURN_LIMIT = 60 * 2**20
SCALARS = pl.BlockSpec(memory_space=pltpu.SMEM)
WHOLE = pl.BlockSpec(memory_space=pltpu.VMEM)
IN_HBM = pl.BlockSpec(memory_space=pltpu.HBM)
ANY = pl.BlockSpec(memory_space=pl.ANY)


def cost(flops, moved):
    return pl.CostEstimate(flops=flops, bytes_accessed=moved, transcendentals=0)


def swap_cores(v):
    return lax.ppermute(v, C, [(0, 1), (1, 0)])


def permute(v, axes, sizes, move):
    count = 1
    for size in sizes:
        count *= size
    pairs = []
    for at in range(count):
        place, rest = [], at
        for size in reversed(sizes):
            place.insert(0, rest % size)
            rest //= size
        to = 0
        for index, size in zip(move(*place), sizes):
            to = to * size + index
        pairs.append((at, to))
    return lax.ppermute(v, axes, pairs)


def on_ring(y, h, steps):
    at = (h * NY + y + steps) % (NH * NY)
    return at % NY, at // NY


def to_neighbours(v):
    return permute(
        v, (Y, H, C), (NY, NH, NC), lambda y, h, c: (*on_ring(y, h, 1 - 2 * c), c)
    )


def to_across(v):
    return permute(
        v, (Y, H), (NY, NH), lambda y, h: on_ring(y, h, 2 if y % 2 == 0 else -2)
    )


def transpose_planes(v, flip):
    pairs = []
    for z in range(NZ):
        for t in range(NX * NH):
            pairs.append((z * NX * NH + t, t * NX * NH + (z ^ flip)))
    return lax.ppermute(v, (Z, X, H), pairs)


def copies_kernel(late_ref, v_ref, out_ref):
    del late_ref
    for i in range(out_ref.shape[0]):
        out_ref[i] = v_ref[...]


def spread_z(v, late):
    copies = pl.pallas_call(
        copies_kernel,
        out_shape=jax.ShapeDtypeStruct((NZ,) + v.shape, v.dtype),
        in_specs=[ANY, WHOLE],
        out_specs=WHOLE,
        cost_estimate=cost(0, 2 * (NZ + 1) * v.size),
        compiler_params=pltpu.CompilerParams(vmem_limit_bytes=VMEM_LIMIT),
    )(late, v)
    return lax.all_to_all(copies, Z, 0, 0)


def cut_kernel(at_ref, values_ref, own_ref, near_ref, across_ref):
    y, core = at_ref[0], at_ref[1]
    width = own_ref.shape[2] // 2
    for z in range(2):
        out = slice(z * width, (z + 1) * width)
        for steps, out_ref in ((0, own_ref), (1 + 2 * core, near_ref), (2, across_ref)):
            block = z * NY + lax.rem(y + steps, NY)
            cols = pl.ds(pl.multiple_of(block * width, width), width)
            if out_ref is across_ref:
                out_ref[:, out] = values_ref[core, :, cols]
            else:
                out_ref[:, :, out] = values_ref[:, :, cols]


def cut_features(at, values):
    seqs, tokens, features = values.shape
    steps = NZ // 2
    part = features // NY // steps
    both = jax.ShapeDtypeStruct((seqs, tokens, features // NY), values.dtype)
    both_spec = pl.BlockSpec((seqs, tokens, part), lambda i: (0, 0, i))
    return pl.pallas_call(
        cut_kernel,
        grid=(steps,),
        out_shape=(both, both, jax.ShapeDtypeStruct((tokens, features // NY), values.dtype)),
        in_specs=[SCALARS, pl.BlockSpec((seqs, tokens, part * NY), lambda i: (0, 0, i))],
        out_specs=(both_spec, both_spec, pl.BlockSpec((tokens, part), lambda i: (0, i))),
        cost_estimate=cost(0, 4 * values.size),
        compiler_params=pltpu.CompilerParams(vmem_limit_bytes=VMEM_LIMIT),
    )(at, values)


def move_tokens(at, values):
    own, near, across = cut_features(at, values)
    return own, [to_neighbours(near), to_across(across)]


def turn_kernel(lates, at_ref, *refs):
    own_ref, near, across, near_other, across_other, basis_ref = refs[lates : lates + 6]
    *outs, rows, basis, sems = refs[lates + 6 :]
    y, core = at_ref[0], at_ref[1]
    tokens = own_ref.shape[1]
    copies = [
        pltpu.make_async_copy(own_ref, rows.at[0:2], sems.at[0]),
        pltpu.make_async_copy(near, rows.at[2:4], sems.at[1]),
        pltpu.make_async_copy(near_other, rows.at[4:6], sems.at[2]),
        pltpu.make_async_copy(across, rows.at[6], sems.at[3]),
        pltpu.make_async_copy(across_other, rows.at[7], sems.at[4]),
        pltpu.make_async_copy(basis_ref, basis, sems.at[5]),
    ]
    for copy in copies:
        copy.start()
    for copy in copies:
        copy.wait()
    product = jnp.dot(
        rows[...].reshape(8 * tokens, rows.shape[2]),
        basis[...],
        preferred_element_type=jnp.float32,
    )
    parts = outs[0].shape[2]
    if parts == 1:
        columns = [product]
    else:
        half = outs[0].shape[5] // 2
        columns = []
        for c in range(parts):
            halves = [
                product[:, (parts * q + c) * half : (parts * q + c + 1) * half]
                for q in range(2)
            ]
            columns.append(jnp.concatenate(halves, axis=1))
    back, on = lax.rem(y + 3 - 2 * core, NY), lax.rem(y + 1 + 2 * core, NY)
    two = lax.rem(y + 2, NY)
    places = [(0, y), (1, y), (0, back), (1, back), (0, on), (1, on), (core, two), (1 - core, two)]
    for i, (seq, source) in enumerate(places):
        for c in range(parts):
            value = columns[c][i * tokens : (i + 1) * tokens]
            for out_ref in outs:
                out_ref[seq, source // 2, c, lax.rem(source, 2)] = value.astype(out_ref.dtype)


def turn(at, late, own, pieces, basis, parts, dtypes):
    seqs, tokens, features = own.shape
    cols = basis.shape[1]
    shape = (seqs, 2, parts, 2, tokens, cols // parts)
    outs = pl.pallas_call(
        lambda *refs: turn_kernel(len(late), *refs),
        out_shape=tuple(jax.ShapeDtypeStruct(shape, dtype) for dtype in dtypes),
        in_specs=[SCALARS] + [ANY] * (2 + len(late) + len(pieces)),
        out_specs=(WHOLE,) * len(dtypes),
        scratch_shapes=[
            pltpu.VMEM((8, tokens, features), own.dtype),
            pltpu.VMEM((features, cols), basis.dtype),
            pltpu.SemaphoreType.DMA((6,)),
        ],
        cost_estimate=cost(
            16 * tokens * features * cols,
            2 * (8 * tokens + cols) * features + 32 * tokens * cols,
        ),
        compiler_params=pltpu.CompilerParams(
            vmem_limit_bytes=TURN_LIMIT if parts > 1 else VMEM_LIMIT
        ),
    )(at, *late, own, *pieces, basis)
    return [out.reshape(NY * parts, 2 * tokens, cols // parts) for out in outs]


def round_kernel(late_ref, v_ref, out_ref):
    del late_ref
    out_ref[...] = v_ref[...].astype(out_ref.dtype)


def rounded(late, v):
    return pl.pallas_call(
        round_kernel,
        out_shape=jax.ShapeDtypeStruct(v.shape, jnp.bfloat16),
        in_specs=[ANY, WHOLE],
        out_specs=WHOLE,
        cost_estimate=cost(0, 6 * v.size),
        compiler_params=pltpu.CompilerParams(vmem_limit_bytes=VMEM_LIMIT),
    )(late, v)


def sum_acts_kernel(at_ref, full_ref, got_ref, out_ref):
    y, core = at_ref[0], at_ref[1]
    totals = []
    for c in range(NC):
        own = NC * y + c
        total = jnp.where(core == c, full_ref[own], got_ref[own].astype(jnp.float32))
        for steps in range(1, NY):
            source = NC * lax.rem(y + steps, NY) + c
            total = total + got_ref[source].astype(jnp.float32)
        totals.append(total)
    out_ref[...] = jnp.concatenate(totals, axis=1).astype(out_ref.dtype)


def sum_acts(at, full, got):
    _, rows, cols = full.shape
    return pl.pallas_call(
        sum_acts_kernel,
        out_shape=jax.ShapeDtypeStruct((rows, NC * cols), jnp.bfloat16),
        in_specs=[SCALARS, WHOLE, WHOLE],
        out_specs=WHOLE,
        cost_estimate=cost(full.size, 4 * full.size + 2 * got.size),
        compiler_params=pltpu.CompilerParams(vmem_limit_bytes=VMEM_LIMIT),
    )(at, full, got)


def sum_grads_kernel(late_ref, got_ref, out_ref):
    del late_ref
    total = got_ref[0] + got_ref[1] + got_ref[2] + got_ref[3]
    out_ref[...] = total


def sum_grads(late, got):
    return pl.pallas_call(
        sum_grads_kernel,
        out_shape=jax.ShapeDtypeStruct(got.shape[1:], got.dtype),
        in_specs=[ANY, WHOLE],
        out_specs=WHOLE,
        cost_estimate=cost(got.size, 5 * got.size),
        compiler_params=pltpu.CompilerParams(vmem_limit_bytes=VMEM_LIMIT),
    )(late, got)


def pair_kernel(at_ref, near_ref, far_ref, out_ref):
    even = at_ref[2] == 0
    near, far = near_ref[...], far_ref[...]
    first, second = jnp.where(even, near, far), jnp.where(even, far, near)
    for i in range(NX):
        out_ref[i, 0] = first
        out_ref[i, 1] = second


def paired(at, near, far):
    return pl.pallas_call(
        pair_kernel,
        out_shape=jax.ShapeDtypeStruct((NX, 2) + near.shape, near.dtype),
        in_specs=[SCALARS, WHOLE, WHOLE],
        out_specs=WHOLE,
        cost_estimate=cost(0, 20 * near.size),
        compiler_params=pltpu.CompilerParams(vmem_limit_bytes=VMEM_LIMIT),
    )(at, near, far)


def outer_kernel(at_ref, acts_ref, mine_ref, other_ref, out_ref):
    core = at_ref[1]
    quarter = out_ref.shape[2]
    for grads_ref, place in ((mine_ref, core), (other_ref, 1 - core)):
        product = lax.dot_general(
            acts_ref[...],
            grads_ref[...].astype(acts_ref.dtype),
            (((0,), (0,)), ((), ())),
            preferred_element_type=jnp.float32,
        ).astype(out_ref.dtype)
        for q in range(NY):
            out_ref[q, place] = product[q * quarter : (q + 1) * quarter]


def outer_product(at, acts, mine, other):
    quarter, cols = acts.shape[1] // NY, mine.shape[1]
    out = pl.pallas_call(
        outer_kernel,
        out_shape=jax.ShapeDtypeStruct((NY, NC, quarter, cols), jnp.bfloat16),
        in_specs=[SCALARS] + [WHOLE] * 3,
        out_specs=WHOLE,
        cost_estimate=cost(
            4 * acts.size * mine.shape[1], 2 * (acts.size + 2 * mine.size) + 2 * NY * NC * quarter * cols
        ),
        compiler_params=pltpu.CompilerParams(vmem_limit_bytes=VMEM_LIMIT),
    )(at, acts, mine, other)
    return out.reshape(NY * NC, quarter, cols)


def local(activations, out_grads, act_basis, grad_basis):
    at = jnp.stack([lax.axis_index(a) for a in (Y, C, H)]).astype(jnp.int32)
    act_cols, grad_cols = act_basis.shape[1], grad_basis.shape[1]
    act_rows = lax.all_gather(act_basis, Z, axis=0, tiled=True)

    grad_rows = spread_z(grad_basis, at).reshape(-1, grad_cols)
    grad_own, grad_pieces = move_tokens(at, out_grads)
    act_own, act_pieces = move_tokens(at, activations)
    grad_pieces = grad_pieces + [swap_cores(v) for v in grad_pieces]

    (grad_part,) = turn(at, act_pieces, grad_own, grad_pieces, grad_rows, 1, [jnp.float32])
    grad_got = lax.all_to_all(grad_part, Y, 0, 0)
    act_pieces = act_pieces + [swap_cores(v) for v in act_pieces]
    act_part, act_send = turn(
        at, [grad_part], act_own, act_pieces, act_rows, NC, [jnp.float32, jnp.bfloat16]
    )
    act_got = lax.all_to_all(act_send, (Y, C), 0, 0)

    grad_turned = sum_grads(act_part, grad_got)
    grad_panel = lax.all_gather(grad_turned, Z, axis=0, tiled=True)

    act_turned = sum_acts(at, act_part, act_got)
    near, far = transpose_planes(act_turned, 0), transpose_planes(act_turned, 1)
    pair = paired(at, near, far)
    act_panel = lax.all_to_all(pair, X, 0, 0).reshape(-1, act_cols)
    grad_panel = rounded(pair, grad_panel)

    outer = outer_product(at, act_panel, grad_panel, swap_cores(grad_panel))
    got = lax.all_to_all(outer, (Y, C), 0, 0).astype(jnp.float32)
    got = got.reshape(NY, -1, got.shape[2])
    first, second = got[0] + got[1], got[2] + got[3]
    count = activations.shape[0] * activations.shape[1] * NZ * NY
    return ((first * first + second * second) / count).T


def solution(mesh):
    fine = Mesh(mesh.devices.reshape(NZ, NY, NX, NH, NC), (Z, Y, X, H, C))
    dp, tensor = (Z, Y), (X, H, C)
    placed = (P(None, dp, None), P(None, dp, None), P(dp, tensor), P(dp, tensor))
    return jax.shard_map(
        local, mesh=fine, in_specs=placed, out_specs=P(tensor, dp), check_vma=False
    )
```
